256 devices in a mesh: acq: 64 (over z, x, core), rng: 4 (over y).
Axes of the slice: x: 4, y: 4, z: 8, core: 2. Of those that a mesh axis runs over, the one named last changes fastest.
Arguments:
- scenes: bfloat16 [128, 2, 256, 8192], P('acq', None, None, 'rng'), may hold values from -30 to 30, as said below
- pairs: int32 [384, 2], P('acq'), may hold values from 0 to 127, as said below
- pair_owner: int32 [384], replicated, may hold values from 0 to 383, each once
- design_pinv: float32 [128, 384], replicated, may hold values from -0.3125 to 0.3125
Outputs:
- series: float32 [64, 128, 512], P('acq', None, 'rng')
The draws below stay inside these ranges and needn't reach their ends.
Inputs may be any that keep to these rules, and one draw needn't show every extreme that they name: Rows d * 6 to (d + 1) * 6 - 1 hold distinct pairs whose two acquisitions lie between (d - 1) * 2 and (d + 2) * 2 - 1, the reference lower than the secondary. `scenes`: every pixel's phase atan2(imaginary, real) lies within -0.75 to 0.75, its magnitude between 0.1 and 30.
All inputs are finite; a program needn't handle non-finite values.
Results may differ from the reference program's by a relative error of at most 0.0003.
Values may be sent and summed in bfloat16 or wider, within the bound.
No kernel may reach another device: no remote copies, remote signals or barrier semaphores. Data moves between devices by JAX's collectives and lax.ppermute only.
A program may use at most 128 MiB of HBM per device.

```python
import jax
import jax.numpy as jnp
import numpy as np
from jax import lax

ACQ_DEV = 2
PAIR_DEV = 6
LOOK_R = 4
LOOK_C = 16
ACQ = 128
PAIRS = 384
ROWS = 256
COLS = 8192
N_ACQ = 64


def draw_scenes(key, part):
    key = jax.random.fold_in(key, 11)
    amp_key, phase_key = jax.random.split(key, 2)
    shape = (ACQ, ROWS, COLS)
    magnitude = jnp.exp(jax.random.uniform(amp_key, shape, jnp.float32, jnp.log(0.3), jnp.log(3.0)))
    angle = jnp.clip(0.3 * jax.random.normal(phase_key, shape, jnp.float32), -0.75, 0.75)
    stacked = jnp.stack([magnitude * jnp.cos(angle), magnitude * jnp.sin(angle)], axis=1)
    return stacked.astype(jnp.bfloat16)


def draw_pairs(key, part):
    key = jax.random.fold_in(key, 5)
    lower, upper = np.triu_indices(3 * ACQ_DEV, 1)
    count = lower.shape[0]
    base = jnp.arange(N_ACQ, dtype=jnp.int32)[:, None] * ACQ_DEV - ACQ_DEV
    first = base + jnp.asarray(lower, jnp.int32)[None, :]
    second = base + jnp.asarray(upper, jnp.int32)[None, :]
    valid = (first >= 0) & (second < ACQ)
    scores = jax.random.randint(key, (N_ACQ, count), 0, 2 ** 20) * count + jnp.arange(count, dtype=jnp.int32)[None, :]
    scores = jnp.where(valid, scores, -1)
    picked = lax.top_k(scores, PAIR_DEV)[1]
    chosen_first = jnp.take_along_axis(first, picked, axis=1)
    chosen_second = jnp.take_along_axis(second, picked, axis=1)
    return jnp.stack([chosen_first, chosen_second], axis=-1).reshape(N_ACQ * PAIR_DEV, 2).astype(jnp.int32)


def normal_values(own_key, dims, width, limit, kind=jnp.bfloat16):
    return jnp.clip(width * jax.random.normal(own_key, dims, jnp.float32), -limit, limit).astype(kind)


def setup_inputs(seed: int = 0) -> dict:
    streams_of = jax.random.split(jax.random.key(seed), 5)
    scenes = draw_scenes(jax.random.fold_in(streams_of[4], 71), 0)
    pairs = draw_pairs(jax.random.fold_in(streams_of[4], 71), 0)
    pair_owner = jax.random.permutation(streams_of[2], PAIRS).astype(jnp.int32)
    design_pinv = normal_values(streams_of[3], (ACQ, PAIRS), PAIRS ** -0.5, 0.3125, jnp.float32)
    return {"scenes": scenes, "pairs": pairs, "pair_owner": pair_owner, "design_pinv": design_pinv}


def multilook(values):
    rows, cols = values.shape
    return values.reshape(rows // LOOK_R, LOOK_R, cols // LOOK_C, LOOK_C).sum(axis=(1, 3))


def reference(scenes, pairs, pair_owner, design_pinv):
    def one_pair(pair):
        first = lax.dynamic_index_in_dim(scenes, pair[0], 0, keepdims=False).astype(jnp.float32)
        second = lax.dynamic_index_in_dim(scenes, pair[1], 0, keepdims=False).astype(jnp.float32)
        real_part = first[0] * second[0] + first[1] * second[1]
        imag_part = first[1] * second[0] - first[0] * second[1]
        return jnp.arctan2(multilook(imag_part), multilook(real_part))

    phase = lax.map(one_pair, pairs)
    slot_pinv = jnp.take(design_pinv, pair_owner, axis=1)
    return jnp.einsum("ap,prc->rac", slot_pinv, phase, precision=lax.Precision.HIGHEST)
```

```python
import functools

import jax
import jax.numpy as jnp
import numpy as np
from jax import lax
from jax.experimental import pallas as pl
from jax.experimental.pallas import tpu as pltpu
from jax.sharding import PartitionSpec as P

LOOK_R = 4
LOOK_C = 16
LANES = 128
CHUNKS = 4
SLOT_PAD = 8
HIGHEST = lax.Precision.HIGHEST

ATAN = (
    0.0030499680532062342, -0.016827448459262765, 0.04385559893448732,
    -0.07596809856148054, 0.1068142102724691, -0.14213196195363814,
    0.19993716142481088, -0.33333120780995057, 0.9999999880828068,
)


def atan_ratio(imag, real):
    size = jnp.abs(imag)
    steep = size > real
    ratio = jnp.minimum(size, real) / jnp.maximum(size, real)
    square = ratio * ratio
    poly = jnp.full_like(square, ATAN[0])
    for coefficient in ATAN[1:]:
        poly = poly * square + coefficient
    angle = poly * ratio
    angle = jnp.where(steep, np.float32(np.pi / 2) - angle, angle)
    return jnp.where(imag < 0, -angle, angle)


def phase_kernel(pairs_ref, low_ref, own_ref, high_ref, ones_ref, out_ref, stack, sums):
    pair_count = pairs_ref.shape[0]
    acq = own_ref.shape[0]
    rows = own_ref.shape[2]
    looked = rows // LOOK_R
    blocks = own_ref.shape[3] // LANES

    def column_block(j, carry):
        lanes = pl.ds(pl.multiple_of(j * LANES, LANES), LANES)
        for side, ref in enumerate((low_ref, own_ref, high_ref)):
            for a in range(acq):
                for part in range(2):
                    stack[side * acq + a, part] = ref[a, part, :, lanes].astype(jnp.float32)
        for p in range(pair_count):
            first, second = pairs_ref[p, 0], pairs_ref[p, 1]
            real = imag = None
            for i in range(LOOK_R):
                pick = pl.ds(i, looked, stride=LOOK_R)
                ar, ai = stack[first, 0, pick, :], stack[first, 1, pick, :]
                cr, ci = stack[second, 0, pick, :], stack[second, 1, pick, :]
                re, im = ar * cr + ai * ci, ai * cr - ar * ci
                real = re if real is None else real + re
                imag = im if imag is None else imag + im
            sums[pl.ds(p * looked, looked), lanes] = real
            sums[pl.ds((pair_count + p) * looked, looked), lanes] = imag
        return carry

    lax.fori_loop(0, blocks, column_block, 0)
    both = jnp.dot(sums[...], ones_ref[...], precision=HIGHEST, preferred_element_type=jnp.float32)
    half = pair_count * looked
    angle = atan_ratio(both[half:], both[:half])
    out_ref[...] = jnp.zeros_like(out_ref)
    for p in range(pair_count):
        out_ref[:, p, :] = angle[p * looked : (p + 1) * looked]


def chunk_phase(pairs, low, scenes, high, ones, k):
    acq, parts, rows, cols = low.shape
    looked = rows // LOOK_R
    pair_count = pairs.shape[0]
    whole = pl.BlockSpec((acq, parts, rows, cols), lambda i: (0, 0, 0, 0))
    return pl.pallas_call(
        phase_kernel,
        grid=(1,),
        out_shape=jax.ShapeDtypeStruct((looked, SLOT_PAD, cols // LOOK_C), jnp.float32),
        in_specs=[
            pl.BlockSpec(memory_space=pltpu.SMEM),
            whole,
            pl.BlockSpec((acq, parts, rows, cols), lambda i: (0, 0, k, 0)),
            whole,
            pl.BlockSpec((cols, cols // LOOK_C), lambda i: (0, 0)),
        ],
        out_specs=pl.BlockSpec((looked, SLOT_PAD, cols // LOOK_C), lambda i: (0, 0, 0)),
        scratch_shapes=[
            pltpu.VMEM((3 * acq, parts, rows, LANES), jnp.float32),
            pltpu.VMEM((2 * pair_count * looked, cols), jnp.float32),
        ],
        compiler_params=pltpu.CompilerParams(vmem_limit_bytes=48 * 2**20),
        name="pair_phase",
    )(pairs, low, scenes, high, ones)


def slots_kernel(owner_ref, pinv_ref, out_ref):
    count = pinv_ref.shape[1]
    row = lax.broadcasted_iota(jnp.int32, (count, owner_ref.shape[1]), 0)
    pick = (row == owner_ref[...]).astype(jnp.float32)
    out_ref[...] = jnp.dot(pinv_ref[...], pick, precision=HIGHEST, preferred_element_type=jnp.float32)


def series_kernel(slots_ref, phase_ref, out_ref):
    phase = phase_ref[...].reshape(slots_ref.shape[1], phase_ref.shape[2])
    out_ref[...] = jnp.dot(
        slots_ref[...], phase, precision=HIGHEST, preferred_element_type=jnp.float32
    )[None]


def body(scenes, pairs, pair_owner, design_pinv):
    acq, parts, rows, cols = scenes.shape
    pair_count = pairs.shape[0]
    count = lax.axis_size("acq")
    local = pairs - (lax.axis_index("acq") - 1) * acq
    forward = [(i, i + 1) for i in range(count - 1)]
    backward = [(t, s) for s, t in forward]
    ones = (
        lax.broadcasted_iota(jnp.int32, (cols, cols // LOOK_C), 0) // LOOK_C
        == lax.broadcasted_iota(jnp.int32, (cols, cols // LOOK_C), 1)
    ).astype(jnp.float32)

    owner = jnp.pad(pair_owner.reshape(count, pair_count), ((0, 0), (0, SLOT_PAD - pair_count)), constant_values=-1)
    slots = pl.pallas_call(
        slots_kernel,
        out_shape=jax.ShapeDtypeStruct((design_pinv.shape[0], count * SLOT_PAD), jnp.float32),
        name="slot_pinv",
    )(owner.reshape(1, count * SLOT_PAD), design_pinv)

    step = rows // CHUNKS
    phases = []
    for k in range(CHUNKS):
        chunk = lax.slice_in_dim(scenes, k * step, (k + 1) * step, axis=2)
        low = lax.ppermute(chunk, "acq", forward)
        high = lax.ppermute(chunk, "acq", backward)
        phases.append(chunk_phase(local, low, scenes, high, ones, k))
    phase = jnp.concatenate(phases, axis=0)
    phase = lax.all_to_all(phase, "acq", split_axis=0, concat_axis=0)
    return pl.pallas_call(
        series_kernel,
        out_shape=jax.ShapeDtypeStruct((1, slots.shape[0], phase.shape[2]), jnp.float32),
        name="series",
    )(slots, phase)


def solution(mesh):
    placed = (P("acq", None, None, "rng"), P("acq", None), P(), P())
    return jax.shard_map(
        body, mesh=mesh, in_specs=placed, out_specs=P("acq", None, "rng"), check_vma=False
    )
```

```python
import jax
import jax.numpy as jnp
import numpy as np
from jax import lax
from jax.experimental import pallas as pl
from jax.experimental.pallas import tpu as pltpu
from jax.sharding import PartitionSpec as P

LOOK_R = 4
LOOK_C = 16
LANES = 128
CHUNKS = (64, 64, 96, 32)
SLOT_PAD = 8
UNROLL_A = 2
UNROLL_B = 2

ATAN = (
    0.0030499680532062342, -0.016827448459262765, 0.04385559893448732,
    -0.07596809856148054, 0.1068142102724691, -0.14213196195363814,
    0.19993716142481088, -0.33333120780995057, 0.9999999880828068,
)


def atan_ratio(imag, real):
    size = jnp.abs(imag)
    steep = size > real
    ratio = jnp.minimum(size, real) / jnp.maximum(size, real)
    square = ratio * ratio
    poly = jnp.full_like(square, ATAN[0])
    for coefficient in ATAN[1:]:
        poly = poly * square + coefficient
    angle = poly * ratio
    angle = jnp.where(steep, np.float32(np.pi / 2) - angle, angle)
    return jnp.where(imag < 0, -angle, angle)


def cut_kernel(scenes_ref, *refs):
    *outs, sems = refs
    copies, start = [], 0
    for k, out in enumerate(outs):
        rows = out.shape[2]
        copy = pltpu.make_async_copy(scenes_ref.at[:, :, pl.ds(start, rows), :], out, sems.at[k])
        copy.start()
        copies.append(copy)
        start += rows
    for copy in copies:
        copy.wait()


def cut_rows(scenes):
    acq, parts, _, cols = scenes.shape
    anywhere = pl.BlockSpec(memory_space=pl.ANY)
    return pl.pallas_call(
        cut_kernel,
        out_shape=[jax.ShapeDtypeStruct((acq, parts, rows, cols), scenes.dtype) for rows in CHUNKS],
        in_specs=[anywhere],
        out_specs=[anywhere] * len(CHUNKS),
        scratch_shapes=[pltpu.SemaphoreType.DMA((len(CHUNKS),))],
        name="cut_rows",
    )(scenes)


def split(x):
    high = x.astype(jnp.bfloat16)
    rest = x - high.astype(jnp.float32)
    mid = rest.astype(jnp.bfloat16)
    return high, mid, (rest - mid.astype(jnp.float32)).astype(jnp.bfloat16)


def phase_kernel(pairs_ref, low_ref, own_ref, high_ref, ones_ref, *refs):
    *earlier, out_ref, stack, sums = refs
    pair_count = pairs_ref.shape[0]
    acq, _, rows, cols = own_ref.shape
    looked = rows // LOOK_R
    blocks = cols // LANES

    def widen(j, carry):
        lanes = pl.ds(pl.multiple_of(j * LANES, LANES), LANES)
        for side, ref in enumerate((low_ref, own_ref, high_ref)):
            for a in range(acq):
                for part in range(2):
                    stack[side * acq + a, part, j] = ref[a, part, :, lanes].astype(jnp.float32)
        return carry

    lax.fori_loop(0, blocks, widen, 0, unroll=UNROLL_A)
    picks = [(pairs_ref[p, 0], pairs_ref[p, 1]) for p in range(pair_count)]

    def form(j, carry):
        lanes = pl.ds(pl.multiple_of(j * LANES, LANES), LANES)
        for p, (first, second) in enumerate(picks):
            real = imag = None
            for i in range(LOOK_R):
                pick = pl.ds(i, looked, stride=LOOK_R)
                ar, ai = stack[first, 0, j, pick, :], stack[first, 1, j, pick, :]
                cr, ci = stack[second, 0, j, pick, :], stack[second, 1, j, pick, :]
                re, im = ar * cr + ai * ci, ai * cr - ar * ci
                real = re if real is None else real + re
                imag = im if imag is None else imag + im
            for piece, value in enumerate(split(jnp.concatenate([real, imag], axis=0))):
                sums[piece, pl.ds(p * 2 * looked, 2 * looked), lanes] = value
        return carry

    lax.fori_loop(0, blocks, form, 0, unroll=UNROLL_B)
    pieces = sums[...].reshape(3 * sums.shape[1], cols)
    dots = jnp.dot(pieces, ones_ref[...], preferred_element_type=jnp.float32)
    dots = dots.reshape(3, pair_count, 2, looked, dots.shape[1])
    both = dots[0] + (dots[1] + dots[2])
    angle = atan_ratio(both[:, 1], both[:, 0])
    start = 0
    for ref in earlier:
        out_ref[pl.ds(start, ref.shape[0])] = ref[...]
        start += ref.shape[0]
    for p in range(pair_count):
        out_ref[pl.ds(start, looked), p, :] = angle[p]
    for p in range(pair_count, SLOT_PAD):
        out_ref[pl.ds(start, looked), p, :] = jnp.zeros_like(angle[0])


def chunk_phase(pairs, low, own, high, ones, earlier=()):
    acq, parts, rows, cols = low.shape
    looked = rows // LOOK_R
    pair_count = pairs.shape[0]
    total = looked + sum(x.shape[0] for x in earlier)
    vmem = pl.BlockSpec(memory_space=pltpu.VMEM)
    return pl.pallas_call(
        phase_kernel,
        out_shape=jax.ShapeDtypeStruct((total, SLOT_PAD, cols // LOOK_C), jnp.float32),
        in_specs=[pl.BlockSpec(memory_space=pltpu.SMEM)] + [vmem] * (4 + len(earlier)),
        out_specs=vmem,
        scratch_shapes=[
            pltpu.VMEM((3 * acq, parts, cols // LANES, rows, LANES), jnp.float32),
            pltpu.VMEM((3, 2 * pair_count * looked, cols), jnp.bfloat16),
        ],
        compiler_params=pltpu.CompilerParams(vmem_limit_bytes=28 * 2**20),
        name="pair_phase",
    )(pairs, low, own, high, ones, *earlier)


def slots_kernel(owner_ref, pinv_ref, out_ref):
    count = pinv_ref.shape[1]
    row = lax.broadcasted_iota(jnp.int32, (count, owner_ref.shape[1]), 0)
    pick = (row == owner_ref[...]).astype(jnp.bfloat16)
    for piece, value in enumerate(split(pinv_ref[...])):
        out_ref[piece] = jnp.dot(value, pick, preferred_element_type=jnp.float32).astype(jnp.bfloat16)


def series_kernel(slots_ref, phase_ref, out_ref):
    acqs, width = slots_ref.shape[1:]
    phase = split(phase_ref[...].reshape(width, phase_ref.shape[2]))
    total = None
    for piece in reversed(range(3)):
        rows = slots_ref[pl.ds(0, 3 - piece)].reshape((3 - piece) * acqs, width)
        dots = jnp.dot(rows, phase[piece], preferred_element_type=jnp.float32)
        for k in reversed(range(3 - piece)):
            part = dots[k * acqs : (k + 1) * acqs]
            total = part if total is None else total + part
    out_ref[0] = total


def body(scenes, pairs, pair_owner, design_pinv):
    acq, parts, rows, cols = scenes.shape
    pair_count = pairs.shape[0]
    count = lax.axis_size("acq")
    local = pairs - (lax.axis_index("acq") - 1) * acq
    forward = [(i, i + 1) for i in range(count - 1)]
    backward = [(t, s) for s, t in forward]

    chunks = cut_rows(scenes)
    halos = [(lax.ppermute(c, "acq", forward), lax.ppermute(c, "acq", backward)) for c in chunks]

    ones = (
        lax.broadcasted_iota(jnp.int32, (cols, cols // LOOK_C), 0) // LOOK_C
        == lax.broadcasted_iota(jnp.int32, (cols, cols // LOOK_C), 1)
    ).astype(jnp.bfloat16)
    owner = jnp.pad(pair_owner.reshape(count, pair_count), ((0, 0), (0, SLOT_PAD - pair_count)), constant_values=-1)
    slots = pl.pallas_call(
        slots_kernel,
        out_shape=jax.ShapeDtypeStruct((3, design_pinv.shape[0], count * SLOT_PAD), jnp.bfloat16),
        name="slot_pinv",
    )(owner.reshape(1, count * SLOT_PAD), design_pinv)

    phases = []
    for k, (chunk, (low, high)) in enumerate(zip(chunks, halos)):
        if k == 0:
            low, slots = lax.optimization_barrier((low, slots))
        last = k == len(chunks) - 1
        phases.append(chunk_phase(local, low, chunk, high, ones, phases if last else ()))
    phase = lax.all_to_all(phases[-1], "acq", split_axis=0, concat_axis=0)
    return pl.pallas_call(
        series_kernel,
        out_shape=jax.ShapeDtypeStruct((1, slots.shape[1], phase.shape[2]), jnp.float32),
        name="series",
    )(slots, phase)


def solution(mesh):
    placed = (P("acq", None, None, "rng"), P("acq", None), P(), P())
    return jax.shard_map(
        body, mesh=mesh, in_specs=placed, out_specs=P("acq", None, "rng"), check_vma=False
    )
```

```python
import jax
import jax.numpy as jnp
import numpy as np
from jax import lax
from jax.experimental import pallas as pl
from jax.experimental.pallas import tpu as pltpu
from jax.sharding import PartitionSpec as P

LOOK_R = 4
LOOK_C = 16
LANES = 128
CHUNKS = (64, 64, 96, 32)
SLOT_PAD = 8
UNROLL_A = 2
UNROLL_B = 2

ATAN = (
    0.0030499680532062342, -0.016827448459262765, 0.04385559893448732,
    -0.07596809856148054, 0.1068142102724691, -0.14213196195363814,
    0.19993716142481088, -0.33333120780995057, 0.9999999880828068,
)


def atan_ratio(imag, real):
    size = jnp.abs(imag)
    steep = size > real
    ratio = jnp.minimum(size, real) / jnp.maximum(size, real)
    square = ratio * ratio
    poly = jnp.full_like(square, ATAN[0])
    for coefficient in ATAN[1:]:
        poly = poly * square + coefficient
    angle = poly * ratio
    angle = jnp.where(steep, np.float32(np.pi / 2) - angle, angle)
    return jnp.where(imag < 0, -angle, angle)


def cut_kernel(scenes_ref, *outs):
    start = 0
    for out in outs:
        rows = out.shape[2]
        out[...] = scenes_ref[:, :, pl.ds(start, rows), :]
        start += rows


def cut_rows(scenes):
    acq, parts, _, cols = scenes.shape
    vmem = pl.BlockSpec(memory_space=pltpu.VMEM)
    return pl.pallas_call(
        cut_kernel,
        out_shape=[jax.ShapeDtypeStruct((acq, parts, rows, cols), scenes.dtype) for rows in CHUNKS],
        in_specs=[vmem],
        out_specs=[vmem] * len(CHUNKS),
        compiler_params=pltpu.CompilerParams(vmem_limit_bytes=16 * 2**20),
        name="cut_rows",
    )(scenes)


def split(x):
    high = x.astype(jnp.bfloat16)
    rest = x - high.astype(jnp.float32)
    mid = rest.astype(jnp.bfloat16)
    return high, mid, (rest - mid.astype(jnp.float32)).astype(jnp.bfloat16)


def phase_kernel(pairs_ref, low_ref, own_ref, high_ref, ones_ref, *refs):
    *earlier, out_ref, stack, sums = refs
    pair_count = pairs_ref.shape[0]
    acq, _, rows, cols = own_ref.shape
    looked = rows // LOOK_R
    blocks = cols // LANES

    def widen(j, carry):
        lanes = pl.ds(pl.multiple_of(j * LANES, LANES), LANES)
        for side, ref in enumerate((low_ref, own_ref, high_ref)):
            for a in range(acq):
                for part in range(2):
                    stack[side * acq + a, part, j] = ref[a, part, :, lanes].astype(jnp.float32)
        return carry

    lax.fori_loop(0, blocks, widen, 0, unroll=UNROLL_A)
    picks = [(pairs_ref[p, 0], pairs_ref[p, 1]) for p in range(pair_count)]

    def form(j, carry):
        lanes = pl.ds(pl.multiple_of(j * LANES, LANES), LANES)
        for p, (first, second) in enumerate(picks):
            real = imag = None
            for i in range(LOOK_R):
                pick = pl.ds(i, looked, stride=LOOK_R)
                ar, ai = stack[first, 0, j, pick, :], stack[first, 1, j, pick, :]
                cr, ci = stack[second, 0, j, pick, :], stack[second, 1, j, pick, :]
                re, im = ar * cr + ai * ci, ai * cr - ar * ci
                real = re if real is None else real + re
                imag = im if imag is None else imag + im
            for piece, value in enumerate(split(jnp.concatenate([real, imag], axis=0))):
                sums[piece, pl.ds(p * 2 * looked, 2 * looked), lanes] = value
        return carry

    lax.fori_loop(0, blocks, form, 0, unroll=UNROLL_B)
    pieces = sums[...].reshape(3 * sums.shape[1], cols)
    dots = jnp.dot(pieces, ones_ref[...], preferred_element_type=jnp.float32)
    dots = dots.reshape(3, pair_count, 2, looked, dots.shape[1])
    both = dots[0] + (dots[1] + dots[2])
    angle = atan_ratio(both[:, 1], both[:, 0])
    start = 0
    for ref in earlier:
        out_ref[pl.ds(start, ref.shape[0])] = ref[...]
        start += ref.shape[0]
    for p in range(pair_count):
        out_ref[pl.ds(start, looked), p, :] = angle[p]
    for p in range(pair_count, SLOT_PAD):
        out_ref[pl.ds(start, looked), p, :] = jnp.zeros_like(angle[0])


def chunk_phase(pairs, low, own, high, ones, earlier=()):
    acq, parts, rows, cols = low.shape
    looked = rows // LOOK_R
    pair_count = pairs.shape[0]
    total = looked + sum(x.shape[0] for x in earlier)
    vmem = pl.BlockSpec(memory_space=pltpu.VMEM)
    return pl.pallas_call(
        phase_kernel,
        out_shape=jax.ShapeDtypeStruct((total, SLOT_PAD, cols // LOOK_C), jnp.float32),
        in_specs=[pl.BlockSpec(memory_space=pltpu.SMEM)] + [vmem] * (4 + len(earlier)),
        out_specs=vmem,
        scratch_shapes=[
            pltpu.VMEM((3 * acq, parts, cols // LANES, rows, LANES), jnp.float32),
            pltpu.VMEM((3, 2 * pair_count * looked, cols), jnp.bfloat16),
        ],
        compiler_params=pltpu.CompilerParams(vmem_limit_bytes=28 * 2**20),
        name="pair_phase",
    )(pairs, low, own, high, ones, *earlier)


def slots_kernel(owner_ref, pinv_ref, out_ref):
    count = pinv_ref.shape[1]
    row = lax.broadcasted_iota(jnp.int32, (count, owner_ref.shape[1]), 0)
    pick = (row == owner_ref[...]).astype(jnp.bfloat16)
    for piece, value in enumerate(split(pinv_ref[...])):
        out_ref[piece] = jnp.dot(value, pick, preferred_element_type=jnp.float32).astype(jnp.bfloat16)


def series_kernel(slots_ref, phase_ref, out_ref):
    acqs, width = slots_ref.shape[1:]
    phase = split(phase_ref[...].reshape(width, phase_ref.shape[2]))
    total = None
    for piece in reversed(range(3)):
        rows = slots_ref[pl.ds(0, 3 - piece)].reshape((3 - piece) * acqs, width)
        dots = jnp.dot(rows, phase[piece], preferred_element_type=jnp.float32)
        for k in reversed(range(3 - piece)):
            part = dots[k * acqs : (k + 1) * acqs]
            total = part if total is None else total + part
    out_ref[0] = total


def body(scenes, pairs, pair_owner, design_pinv):
    acq, parts, rows, cols = scenes.shape
    pair_count = pairs.shape[0]
    count = lax.axis_size("acq")
    local = pairs - (lax.axis_index("acq") - 1) * acq
    forward = [(i, i + 1) for i in range(count - 1)]
    backward = [(t, s) for s, t in forward]

    chunks = cut_rows(scenes)
    halos = []
    for k, chunk in enumerate(chunks):
        if k >= 2:
            chunk, halos[k - 2] = lax.optimization_barrier((chunk, halos[k - 2]))
        halos.append((lax.ppermute(chunk, "acq", forward), lax.ppermute(chunk, "acq", backward)))

    ones = (
        lax.broadcasted_iota(jnp.int32, (cols, cols // LOOK_C), 0) // LOOK_C
        == lax.broadcasted_iota(jnp.int32, (cols, cols // LOOK_C), 1)
    ).astype(jnp.bfloat16)
    owner = jnp.pad(pair_owner.reshape(count, pair_count), ((0, 0), (0, SLOT_PAD - pair_count)), constant_values=-1)
    slots = pl.pallas_call(
        slots_kernel,
        out_shape=jax.ShapeDtypeStruct((3, design_pinv.shape[0], count * SLOT_PAD), jnp.bfloat16),
        name="slot_pinv",
    )(owner.reshape(1, count * SLOT_PAD), design_pinv)

    phases = []
    for k, (chunk, (low, high)) in enumerate(zip(chunks, halos)):
        if k == 0:
            low, slots = lax.optimization_barrier((low, slots))
        last = k == len(chunks) - 1
        phases.append(chunk_phase(local, low, chunk, high, ones, phases if last else ()))
    phase = lax.all_to_all(phases[-1], "acq", split_axis=0, concat_axis=0)
    return pl.pallas_call(
        series_kernel,
        out_shape=jax.ShapeDtypeStruct((1, slots.shape[1], phase.shape[2]), jnp.float32),
        name="series",
    )(slots, phase)


def solution(mesh):
    placed = (P("acq", None, None, "rng"), P("acq", None), P(), P())
    return jax.shard_map(
        body, mesh=mesh, in_specs=placed, out_specs=P("acq", None, "rng"), check_vma=False
    )
```

```python
import functools

import jax
import jax.numpy as jnp
import numpy as np
from jax import lax
from jax.experimental import pallas as pl
from jax.experimental.pallas import tpu as pltpu
from jax.sharding import PartitionSpec as P

LOOK_R = 4
LOOK_C = 16
LANES = 128
CHUNKS = (128, 96, 32)
BAND = 32
SLOT_PAD = 8
UNROLL_A = 2
UNROLL_B = 2

ATAN = (
    0.0030499680532062342, -0.016827448459262765, 0.04385559893448732,
    -0.07596809856148054, 0.1068142102724691, -0.14213196195363814,
    0.19993716142481088, -0.33333120780995057, 0.9999999880828068,
)


def atan_ratio(imag, real):
    size = jnp.abs(imag)
    steep = size > real
    ratio = jnp.minimum(size, real) / jnp.maximum(size, real)
    square = ratio * ratio
    poly = jnp.full_like(square, ATAN[0])
    for coefficient in ATAN[1:]:
        poly = poly * square + coefficient
    angle = poly * ratio
    angle = jnp.where(steep, np.float32(np.pi / 2) - angle, angle)
    return jnp.where(imag < 0, -angle, angle)


def split(x, count):
    pieces = []
    for _ in range(count):
        pieces.append(x.astype(jnp.bfloat16))
        x = x - pieces[-1].astype(jnp.float32)
    return pieces


def phase_kernel(start, pairs_ref, far_ref, own_ref, near_ref, ones_ref, *refs):
    *earlier, out_ref, stack, sums = refs
    pair_count = pairs_ref.shape[0]
    acq, _, rows, cols = far_ref.shape
    bands, looked = rows // BAND, BAND // LOOK_R
    blocks = cols // LANES
    picks = [(pairs_ref[p, 0], pairs_ref[p, 1]) for p in range(pair_count)]

    def band(b, carry):
        own_rows = pl.ds(pl.multiple_of(start + b * BAND, BAND), BAND)
        far_rows = pl.ds(pl.multiple_of(b * BAND, BAND), BAND)

        def widen(j, carry):
            lanes = pl.ds(pl.multiple_of(j * LANES, LANES), LANES)
            for side, (ref, at) in enumerate(((far_ref, far_rows), (own_ref, own_rows), (near_ref, own_rows))):
                for a in range(acq):
                    for part in range(2):
                        stack[side * acq + a, part, j] = ref[a, part, at, lanes].astype(jnp.float32)
            return carry

        def form(j, carry):
            lanes = pl.ds(pl.multiple_of(j * LANES, LANES), LANES)
            for p, (first, second) in enumerate(picks):
                real = imag = None
                for i in range(LOOK_R):
                    pick = pl.ds(i, looked, stride=LOOK_R)
                    ar, ai = stack[first, 0, j, pick, :], stack[first, 1, j, pick, :]
                    cr, ci = stack[second, 0, j, pick, :], stack[second, 1, j, pick, :]
                    re, im = ar * cr + ai * ci, ai * cr - ar * ci
                    real = re if real is None else real + re
                    imag = im if imag is None else imag + im
                for piece, value in enumerate(split(jnp.concatenate([real, imag], axis=0), 2)):
                    sums[piece, b, pl.ds(p * 2 * looked, 2 * looked), lanes] = value
            return carry

        lax.fori_loop(0, blocks, widen, 0, unroll=2)
        lax.fori_loop(0, blocks, form, 0, unroll=2)
        return carry

    lax.fori_loop(0, bands, band, 0)
    pieces = sums[...].reshape(2 * bands * sums.shape[2], cols)
    dots = jnp.dot(pieces, ones_ref[...], preferred_element_type=jnp.float32)
    dots = dots.reshape(2, bands, pair_count, 2, looked, dots.shape[1])
    both = dots[0] + dots[1]
    angle = atan_ratio(both[:, :, 1], both[:, :, 0])
    at = 0
    for ref in earlier:
        out_ref[pl.ds(at, ref.shape[0])] = ref[...]
        at += ref.shape[0]
    for b in range(bands):
        for p in range(SLOT_PAD):
            out_ref[pl.ds(at + b * looked, looked), p, :] = (
                angle[b, p] if p < pair_count else jnp.zeros_like(angle[b, 0])
            )


def chunk_phase(start, pairs, far, own, near, ones, earlier=()):
    acq, parts, rows, cols = far.shape
    looked = rows // LOOK_R
    pair_count = pairs.shape[0]
    total = looked + sum(x.shape[0] for x in earlier)
    vmem = pl.BlockSpec(memory_space=pltpu.VMEM)
    return pl.pallas_call(
        functools.partial(phase_kernel, start),
        out_shape=jax.ShapeDtypeStruct((total, SLOT_PAD, cols // LOOK_C), jnp.float32),
        in_specs=[pl.BlockSpec(memory_space=pltpu.SMEM)] + [vmem] * (4 + len(earlier)),
        out_specs=vmem,
        scratch_shapes=[
            pltpu.VMEM((3 * acq, parts, cols // LANES, BAND, LANES), jnp.float32),
            pltpu.VMEM((2, rows // BAND, 2 * pair_count * BAND // LOOK_R, cols), jnp.bfloat16),
        ],
        compiler_params=pltpu.CompilerParams(vmem_limit_bytes=24 * 2**20),
        name="pair_phase",
    )(pairs, far, own, near, ones, *earlier)


def slots_kernel(owner_ref, pinv_ref, out_ref):
    count = pinv_ref.shape[1]
    row = lax.broadcasted_iota(jnp.int32, (count, owner_ref.shape[1]), 0)
    pick = (row == owner_ref[...]).astype(jnp.bfloat16)
    for piece, value in enumerate(split(pinv_ref[...], 3)):
        out_ref[piece] = jnp.dot(value, pick, preferred_element_type=jnp.float32).astype(jnp.bfloat16)


def series_kernel(slots_ref, phase_ref, out_ref):
    acqs, width = slots_ref.shape[1:]
    phase = split(phase_ref[...].reshape(width, phase_ref.shape[2]), 3)
    total = None
    for piece in reversed(range(3)):
        rows = slots_ref[pl.ds(0, 3 - piece)].reshape((3 - piece) * acqs, width)
        dots = jnp.dot(rows, phase[piece], preferred_element_type=jnp.float32)
        for k in reversed(range(3 - piece)):
            part = dots[k * acqs : (k + 1) * acqs]
            total = part if total is None else total + part
    out_ref[0] = total


def body(scenes, pairs, pair_owner, design_pinv):
    acq, parts, rows, cols = scenes.shape
    pair_count = pairs.shape[0]
    count = lax.axis_size("acq")
    me = lax.axis_index("acq")
    near_pairs = [(i, i ^ 1) for i in range(count)]
    far_pairs = [(i, i + 1 if i % 2 else i - 1) for i in range(1, count - 1)]
    local = pairs - (me - 1) * acq
    local = jnp.where(me % 2 == 1, (2 - local // acq) * acq + local % acq, local)

    chunks, halos, start = [], [], 0
    rest, near = scenes, None
    for k, step in enumerate(CHUNKS):
        chunk = lax.slice_in_dim(rest, start, start + step, axis=2)
        rest, chunk = lax.optimization_barrier((rest, chunk))
        halos.append(lax.ppermute(chunk, "acq", far_pairs))
        chunks.append(start)
        start += step
        if k == 0:
            near = lax.ppermute(rest, "acq", near_pairs)
            rest, near = lax.optimization_barrier((rest, near))
        else:
            rest, halos[k - 1] = lax.optimization_barrier((rest, halos[k - 1]))

    ones = (
        lax.broadcasted_iota(jnp.int32, (cols, cols // LOOK_C), 0) // LOOK_C
        == lax.broadcasted_iota(jnp.int32, (cols, cols // LOOK_C), 1)
    ).astype(jnp.bfloat16)
    owner = jnp.pad(pair_owner.reshape(count, pair_count), ((0, 0), (0, SLOT_PAD - pair_count)), constant_values=-1)
    slots = pl.pallas_call(
        slots_kernel,
        out_shape=jax.ShapeDtypeStruct((3, design_pinv.shape[0], count * SLOT_PAD), jnp.bfloat16),
        name="slot_pinv",
    )(owner.reshape(1, count * SLOT_PAD), design_pinv)

    phases = []
    for k, (start, far) in enumerate(zip(chunks, halos)):
        if k == 0:
            far, slots = lax.optimization_barrier((far, slots))
        last = k == len(chunks) - 1
        phases.append(chunk_phase(start, local, far, scenes, near, ones, phases if last else ()))
    phase = lax.all_to_all(phases[-1], "acq", split_axis=0, concat_axis=0)
    return pl.pallas_call(
        series_kernel,
        out_shape=jax.ShapeDtypeStruct((1, slots.shape[1], phase.shape[2]), jnp.float32),
        name="series",
    )(slots, phase)


def solution(mesh):
    placed = (P("acq", None, None, "rng"), P("acq", None), P(), P())
    return jax.shard_map(
        body, mesh=mesh, in_specs=placed, out_specs=P("acq", None, "rng"), check_vma=False
    )
```

```python
import functools

import jax
import jax.numpy as jnp
import numpy as np
from jax import lax
from jax.experimental import pallas as pl
from jax.experimental.pallas import tpu as pltpu
from jax.sharding import PartitionSpec as P

LOOK_R = 4
LOOK_C = 16
LANES = 128
CHUNKS = (64, 96, 64, 32)
BAND = 32
PHASE_VMEM = 10 * 2**20
SMALL_VMEM = 6 * 2**20
SLOT_PAD = 8
UNROLL_A = 2
UNROLL_B = 2

ATAN = (
    0.0030499680532062342, -0.016827448459262765, 0.04385559893448732,
    -0.07596809856148054, 0.1068142102724691, -0.14213196195363814,
    0.19993716142481088, -0.33333120780995057, 0.9999999880828068,
)


def atan_ratio(imag, real):
    size = jnp.abs(imag)
    steep = size > real
    ratio = jnp.minimum(size, real) / jnp.maximum(size, real)
    square = ratio * ratio
    poly = jnp.full_like(square, ATAN[0])
    for coefficient in ATAN[1:]:
        poly = poly * square + coefficient
    angle = poly * ratio
    angle = jnp.where(steep, np.float32(np.pi / 2) - angle, angle)
    return jnp.where(imag < 0, -angle, angle)


def cut_kernel(start, scenes_ref, *refs):
    *outs, sems = refs
    copies = []
    for k, out in enumerate(outs):
        rows = out.shape[2]
        copies.append(pltpu.make_async_copy(scenes_ref.at[:, :, pl.ds(start, rows), :], out, sems.at[k]))
        start += rows
    for copy in copies:
        copy.start()
    for copy in copies:
        copy.wait()


def cut_rows(scenes, start, sizes):
    acq, parts, _, cols = scenes.shape
    vmem = pl.BlockSpec(memory_space=pltpu.VMEM)
    return pl.pallas_call(
        functools.partial(cut_kernel, start),
        out_shape=[jax.ShapeDtypeStruct((acq, parts, rows, cols), scenes.dtype) for rows in sizes],
        in_specs=[pl.BlockSpec(memory_space=pltpu.HBM)],
        out_specs=[vmem] * len(sizes),
        scratch_shapes=[pltpu.SemaphoreType.DMA((len(sizes),))],
        compiler_params=pltpu.CompilerParams(vmem_limit_bytes=SMALL_VMEM),
        name="cut_rows",
    )(scenes)


def split(x, count):
    pieces = []
    for _ in range(count):
        pieces.append(x.astype(jnp.bfloat16))
        x = x - pieces[-1].astype(jnp.float32)
    return pieces


def phase_kernel(pairs_ref, far_ref, own_ref, near_ref, ones_ref, *refs):
    *earlier, out_ref, stack, sums = refs
    pair_count = pairs_ref.shape[0]
    acq, _, rows, cols = far_ref.shape
    bands, looked = rows // BAND, BAND // LOOK_R
    blocks = cols // LANES
    picks = [(pairs_ref[p, 0], pairs_ref[p, 1]) for p in range(pair_count)]

    def band(b, carry):
        at = pl.ds(pl.multiple_of(b * BAND, BAND), BAND)

        def widen(j, carry):
            lanes = pl.ds(pl.multiple_of(j * LANES, LANES), LANES)
            for side, ref in enumerate((far_ref, own_ref, near_ref)):
                for a in range(acq):
                    for part in range(2):
                        stack[side * acq + a, part, j] = ref[a, part, at, lanes].astype(jnp.float32)
            return carry

        def form(j, carry):
            lanes = pl.ds(pl.multiple_of(j * LANES, LANES), LANES)
            for p, (first, second) in enumerate(picks):
                real = imag = None
                for i in range(LOOK_R):
                    pick = pl.ds(i, looked, stride=LOOK_R)
                    ar, ai = stack[first, 0, j, pick, :], stack[first, 1, j, pick, :]
                    cr, ci = stack[second, 0, j, pick, :], stack[second, 1, j, pick, :]
                    re, im = ar * cr + ai * ci, ai * cr - ar * ci
                    real = re if real is None else real + re
                    imag = im if imag is None else imag + im
                for piece, value in enumerate(split(jnp.concatenate([real, imag], axis=0), 2)):
                    sums[piece, b, pl.ds(p * 2 * looked, 2 * looked), lanes] = value
            return carry

        lax.fori_loop(0, blocks, widen, 0, unroll=2)
        lax.fori_loop(0, blocks, form, 0, unroll=2)
        return carry

    lax.fori_loop(0, bands, band, 0)
    pieces = sums[...].reshape(2 * bands * sums.shape[2], cols)
    dots = jnp.dot(pieces, ones_ref[...], preferred_element_type=jnp.float32)
    dots = dots.reshape(2, bands, pair_count, 2, looked, dots.shape[1])
    both = dots[0] + dots[1]
    angle = atan_ratio(both[:, :, 1], both[:, :, 0])
    at = 0
    for ref in earlier:
        out_ref[pl.ds(at, ref.shape[0])] = ref[...]
        at += ref.shape[0]
    for b in range(bands):
        for p in range(SLOT_PAD):
            out_ref[pl.ds(at + b * looked, looked), p, :] = (
                angle[b, p] if p < pair_count else jnp.zeros_like(angle[b, 0])
            )


def chunk_phase(pairs, far, own, near, ones, earlier=()):
    acq, parts, rows, cols = far.shape
    looked = rows // LOOK_R
    pair_count = pairs.shape[0]
    total = looked + sum(x.shape[0] for x in earlier)
    vmem = pl.BlockSpec(memory_space=pltpu.VMEM)
    return pl.pallas_call(
        phase_kernel,
        out_shape=jax.ShapeDtypeStruct((total, SLOT_PAD, cols // LOOK_C), jnp.float32),
        in_specs=[pl.BlockSpec(memory_space=pltpu.SMEM)] + [vmem] * (4 + len(earlier)),
        out_specs=vmem,
        scratch_shapes=[
            pltpu.VMEM((3 * acq, parts, cols // LANES, BAND, LANES), jnp.float32),
            pltpu.VMEM((2, rows // BAND, 2 * pair_count * BAND // LOOK_R, cols), jnp.bfloat16),
        ],
        compiler_params=pltpu.CompilerParams(vmem_limit_bytes=PHASE_VMEM),
        name="pair_phase",
    )(pairs, far, own, near, ones, *earlier)


def constants_kernel(owner_ref, pinv_ref, slots_ref, ones_ref):
    count = pinv_ref.shape[1]
    row = lax.broadcasted_iota(jnp.int32, (count, owner_ref.shape[1]), 0)
    pick = (row == owner_ref[...]).astype(jnp.bfloat16)
    for piece, value in enumerate(split(pinv_ref[...], 3)):
        slots_ref[piece] = jnp.dot(value, pick, preferred_element_type=jnp.float32).astype(jnp.bfloat16)
    col = lax.broadcasted_iota(jnp.int32, ones_ref.shape, 0) // LOOK_C
    ones_ref[...] = (col == lax.broadcasted_iota(jnp.int32, ones_ref.shape, 1)).astype(jnp.bfloat16)


def series_kernel(slots_ref, phase_ref, out_ref):
    acqs, width = slots_ref.shape[1:]
    phase = split(phase_ref[...].reshape(width, phase_ref.shape[2]), 3)
    total = None
    for piece in reversed(range(3)):
        rows = slots_ref[pl.ds(0, 3 - piece)].reshape((3 - piece) * acqs, width)
        dots = jnp.dot(rows, phase[piece], preferred_element_type=jnp.float32)
        for k in reversed(range(3 - piece)):
            part = dots[k * acqs : (k + 1) * acqs]
            total = part if total is None else total + part
    out_ref[0] = total


def body(scenes, pairs, pair_owner, design_pinv):
    acq, parts, rows, cols = scenes.shape
    pair_count = pairs.shape[0]
    count = lax.axis_size("acq")
    me = lax.axis_index("acq")
    near_pairs = [(i, i ^ 1) for i in range(count)]
    far_pairs = [(i, i + 1 if i % 2 else i - 1) for i in range(1, count - 1)]
    local = pairs - (me - 1) * acq
    local = jnp.where(me % 2 == 1, (2 - local // acq) * acq + local % acq, local)

    owner = jnp.pad(pair_owner.reshape(count, pair_count), ((0, 0), (0, SLOT_PAD - pair_count)), constant_values=-1)
    slots, ones = pl.pallas_call(
        constants_kernel,
        out_shape=[
            jax.ShapeDtypeStruct((3, design_pinv.shape[0], count * SLOT_PAD), jnp.bfloat16),
            jax.ShapeDtypeStruct((cols, cols // LOOK_C), jnp.bfloat16),
        ],
        compiler_params=pltpu.CompilerParams(vmem_limit_bytes=SMALL_VMEM),
        name="constants",
    )(owner.reshape(1, count * SLOT_PAD), design_pinv)

    def swap(chunk):
        return lax.ppermute(chunk, "acq", far_pairs), lax.ppermute(chunk, "acq", near_pairs)

    chunks = [lax.slice_in_dim(scenes, 0, CHUNKS[0], axis=2)]
    halos, phases = [swap(chunks[0])], []
    rest, slots, ones, chunks[0] = lax.optimization_barrier((scenes, slots, ones, chunks[0]))
    chunks += list(cut_rows(rest, CHUNKS[0], CHUNKS[1:]))
    halos.append(swap(chunks[1]))
    for k, chunk in enumerate(chunks):
        far, near = halos[k]
        last = k == len(chunks) - 1
        phases.append(chunk_phase(local, far, chunk, near, ones, phases if last else ()))
        if k + 2 < len(chunks):
            done = phases if k == 0 else halos
            chunks[k + 2], done[k] = lax.optimization_barrier((chunks[k + 2], done[k]))
            halos.append(swap(chunks[k + 2]))
    phase = lax.all_to_all(phases[-1], "acq", split_axis=0, concat_axis=0)
    return pl.pallas_call(
        series_kernel,
        out_shape=jax.ShapeDtypeStruct((1, slots.shape[1], phase.shape[2]), jnp.float32),
        compiler_params=pltpu.CompilerParams(vmem_limit_bytes=SMALL_VMEM),
        name="series",
    )(slots, phase)


def solution(mesh):
    placed = (P("acq", None, None, "rng"), P("acq", None), P(), P())
    return jax.shard_map(
        body, mesh=mesh, in_specs=placed, out_specs=P("acq", None, "rng"), check_vma=False
    )
```

```python
import functools

import jax
import jax.numpy as jnp
import numpy as np
from jax import lax
from jax.experimental import pallas as pl
from jax.experimental.pallas import tpu as pltpu
from jax.sharding import PartitionSpec as P

LOOK_R = 4
LOOK_C = 16
LANES = 128
CHUNKS = (64, 96, 64, 32)
BAND = 32
PHASE_VMEM = 10 * 2**20
SMALL_VMEM = 6 * 2**20
UNROLL_A = 2
UNROLL_B = 2

ATAN = (
    0.0030499680532062342, -0.016827448459262765, 0.04385559893448732,
    -0.07596809856148054, 0.1068142102724691, -0.14213196195363814,
    0.19993716142481088, -0.33333120780995057, 0.9999999880828068,
)


def atan_ratio(imag, real):
    size = jnp.abs(imag)
    steep = size > real
    ratio = jnp.minimum(size, real) / jnp.maximum(size, real)
    square = ratio * ratio
    poly = jnp.full_like(square, ATAN[0])
    for coefficient in ATAN[1:]:
        poly = poly * square + coefficient
    angle = poly * ratio
    angle = jnp.where(steep, np.float32(np.pi / 2) - angle, angle)
    return jnp.where(imag < 0, -angle, angle)


def cut_kernel(start, scenes_ref, *refs):
    *outs, sems = refs
    copies = []
    for k, out in enumerate(outs):
        rows = out.shape[2]
        copies.append(pltpu.make_async_copy(scenes_ref.at[:, :, pl.ds(start, rows), :], out, sems.at[k]))
        start += rows
    for copy in copies:
        copy.start()
    for copy in copies:
        copy.wait()


def cut_rows(scenes, start, sizes):
    acq, parts, _, cols = scenes.shape
    vmem = pl.BlockSpec(memory_space=pltpu.VMEM)
    return pl.pallas_call(
        functools.partial(cut_kernel, start),
        out_shape=[jax.ShapeDtypeStruct((acq, parts, rows, cols), scenes.dtype) for rows in sizes],
        in_specs=[pl.BlockSpec(memory_space=pltpu.HBM)],
        out_specs=[vmem] * len(sizes),
        scratch_shapes=[pltpu.SemaphoreType.DMA((len(sizes),))],
        compiler_params=pltpu.CompilerParams(vmem_limit_bytes=SMALL_VMEM),
        name="cut_rows",
    )(scenes)


def split(x, count):
    pieces = []
    for _ in range(count):
        pieces.append(x.astype(jnp.bfloat16))
        x = x - pieces[-1].astype(jnp.float32)
    return pieces


def phase_kernel(pairs_ref, far_ref, own_ref, near_ref, ones_ref, *refs):
    *earlier, out_ref, stack, sums = refs
    pair_count = pairs_ref.shape[0]
    acq, _, rows, cols = far_ref.shape
    bands, looked = rows // BAND, BAND // LOOK_R
    blocks = cols // LANES
    picks = [(pairs_ref[p, 0], pairs_ref[p, 1]) for p in range(pair_count)]

    def band(b, carry):
        at = pl.ds(pl.multiple_of(b * BAND, BAND), BAND)

        def widen(j, carry):
            lanes = pl.ds(pl.multiple_of(j * LANES, LANES), LANES)
            for side, ref in enumerate((far_ref, own_ref, near_ref)):
                for a in range(acq):
                    for part in range(2):
                        stack[side * acq + a, part, j] = ref[a, part, at, lanes].astype(jnp.float32)
            return carry

        def form(j, carry):
            lanes = pl.ds(pl.multiple_of(j * LANES, LANES), LANES)
            for p, (first, second) in enumerate(picks):
                real = imag = None
                for i in range(LOOK_R):
                    pick = pl.ds(i, looked, stride=LOOK_R)
                    ar, ai = stack[first, 0, j, pick, :], stack[first, 1, j, pick, :]
                    cr, ci = stack[second, 0, j, pick, :], stack[second, 1, j, pick, :]
                    re, im = ar * cr + ai * ci, ai * cr - ar * ci
                    real = re if real is None else real + re
                    imag = im if imag is None else imag + im
                for piece, value in enumerate(split(jnp.concatenate([real, imag], axis=0), 2)):
                    sums[piece, b, pl.ds(p * 2 * looked, 2 * looked), lanes] = value
            return carry

        lax.fori_loop(0, blocks, widen, 0, unroll=2)
        lax.fori_loop(0, blocks, form, 0, unroll=2)
        return carry

    lax.fori_loop(0, bands, band, 0)
    pieces = sums[...].reshape(2 * bands * sums.shape[2], cols)
    dots = jnp.dot(pieces, ones_ref[...], preferred_element_type=jnp.float32)
    dots = dots.reshape(2, bands, pair_count, 2, looked, dots.shape[1])
    both = dots[0] + dots[1]
    width = dots.shape[-1]
    angle = atan_ratio(both[:, :, 1], both[:, :, 0])
    at = 0
    for ref in earlier:
        out_ref[pl.ds(at, ref.shape[0])] = ref[...]
        at += ref.shape[0]
    for b in range(bands):
        for p in range(pair_count):
            out_ref[pl.ds(at + b * looked, looked), 0, pl.ds(p * width, width)] = angle[b, p]


def chunk_phase(pairs, far, own, near, ones, earlier=()):
    acq, parts, rows, cols = far.shape
    looked = rows // LOOK_R
    pair_count = pairs.shape[0]
    total = looked + sum(x.shape[0] for x in earlier)
    vmem = pl.BlockSpec(memory_space=pltpu.VMEM)
    return pl.pallas_call(
        phase_kernel,
        out_shape=jax.ShapeDtypeStruct((total, 1, pair_count * (cols // LOOK_C)), jnp.float32),
        in_specs=[pl.BlockSpec(memory_space=pltpu.SMEM)] + [vmem] * (4 + len(earlier)),
        out_specs=vmem,
        scratch_shapes=[
            pltpu.VMEM((3 * acq, parts, cols // LANES, BAND, LANES), jnp.float32),
            pltpu.VMEM((2, rows // BAND, 2 * pair_count * BAND // LOOK_R, cols), jnp.bfloat16),
        ],
        compiler_params=pltpu.CompilerParams(vmem_limit_bytes=PHASE_VMEM),
        name="pair_phase",
    )(pairs, far, own, near, ones, *earlier)


def constants_kernel(owner_ref, pinv_ref, slots_ref, ones_ref):
    count = pinv_ref.shape[1]
    row = lax.broadcasted_iota(jnp.int32, (count, owner_ref.shape[1]), 0)
    pick = (row == owner_ref[...]).astype(jnp.bfloat16)
    for piece, value in enumerate(split(pinv_ref[...], 3)):
        slots_ref[piece] = jnp.dot(value, pick, preferred_element_type=jnp.float32).astype(jnp.bfloat16)
    col = lax.broadcasted_iota(jnp.int32, ones_ref.shape, 0) // LOOK_C
    ones_ref[...] = (col == lax.broadcasted_iota(jnp.int32, ones_ref.shape, 1)).astype(jnp.bfloat16)


def series_kernel(slots_ref, phase_ref, out_ref):
    acqs, width = slots_ref.shape[1:]
    count, _, lanes = phase_ref.shape
    lanes = lanes * count // width
    phase = [phase_ref[:, 0, pl.ds(p * lanes, lanes)] for p in range(width // count)]
    phase = split(jnp.concatenate(phase, axis=0), 3)
    total = None
    for piece in reversed(range(3)):
        rows = slots_ref[pl.ds(0, 3 - piece)].reshape((3 - piece) * acqs, width)
        dots = jnp.dot(rows, phase[piece], preferred_element_type=jnp.float32)
        for k in reversed(range(3 - piece)):
            part = dots[k * acqs : (k + 1) * acqs]
            total = part if total is None else total + part
    out_ref[0] = total


def body(scenes, pairs, pair_owner, design_pinv):
    acq, parts, rows, cols = scenes.shape
    pair_count = pairs.shape[0]
    count = lax.axis_size("acq")
    me = lax.axis_index("acq")
    near_pairs = [(i, i ^ 1) for i in range(count)]
    far_pairs = [(i, i + 1 if i % 2 else i - 1) for i in range(1, count - 1)]
    local = pairs - (me - 1) * acq
    local = jnp.where(me % 2 == 1, (2 - local // acq) * acq + local % acq, local)

    owner = pair_owner.reshape(count, pair_count).T.reshape(1, count * pair_count)
    slots, ones = pl.pallas_call(
        constants_kernel,
        out_shape=[
            jax.ShapeDtypeStruct((3, design_pinv.shape[0], count * pair_count), jnp.bfloat16),
            jax.ShapeDtypeStruct((cols, cols // LOOK_C), jnp.bfloat16),
        ],
        compiler_params=pltpu.CompilerParams(vmem_limit_bytes=SMALL_VMEM),
        name="constants",
    )(owner, design_pinv)

    def swap(chunk):
        return lax.ppermute(chunk, "acq", far_pairs), lax.ppermute(chunk, "acq", near_pairs)

    chunks = [lax.slice_in_dim(scenes, 0, CHUNKS[0], axis=2)]
    halos, phases = [swap(chunks[0])], []
    rest, slots, ones, chunks[0] = lax.optimization_barrier((scenes, slots, ones, chunks[0]))
    chunks += list(cut_rows(rest, CHUNKS[0], CHUNKS[1:]))
    halos.append(swap(chunks[1]))
    for k, chunk in enumerate(chunks):
        far, near = halos[k]
        last = k == len(chunks) - 1
        phases.append(chunk_phase(local, far, chunk, near, ones, phases if last else ()))
        if k + 2 < len(chunks):
            done = phases if k == 0 else halos
            chunks[k + 2], done[k] = lax.optimization_barrier((chunks[k + 2], done[k]))
            halos.append(swap(chunks[k + 2]))
    phase = lax.all_to_all(phases[-1], "acq", split_axis=0, concat_axis=0)
    return pl.pallas_call(
        series_kernel,
        out_shape=jax.ShapeDtypeStruct((1, slots.shape[1], cols // LOOK_C), jnp.float32),
        compiler_params=pltpu.CompilerParams(vmem_limit_bytes=SMALL_VMEM),
        name="series",
    )(slots, phase)


def solution(mesh):
    placed = (P("acq", None, None, "rng"), P("acq", None), P(), P())
    return jax.shard_map(
        body, mesh=mesh, in_specs=placed, out_specs=P("acq", None, "rng"), check_vma=False
    )
```

```python
import functools

import jax
import jax.numpy as jnp
import numpy as np
from jax import lax
from jax.experimental import pallas as pl
from jax.experimental.pallas import tpu as pltpu
from jax.sharding import PartitionSpec as P

LOOK_R = 4
LOOK_C = 16
LANES = 128
CHUNKS = (64, 96, 64, 32)
BAND = 32
PHASE_VMEM = 10 * 2**20
SMALL_VMEM = 6 * 2**20
UNROLL_A = 2
UNROLL_B = 2

ATAN = (
    0.0030499680532062342, -0.016827448459262765, 0.04385559893448732,
    -0.07596809856148054, 0.1068142102724691, -0.14213196195363814,
    0.19993716142481088, -0.33333120780995057, 0.9999999880828068,
)


def atan_ratio(imag, real):
    size = jnp.abs(imag)
    steep = size > real
    ratio = jnp.minimum(size, real) / jnp.maximum(size, real)
    square = ratio * ratio
    poly = jnp.full_like(square, ATAN[0])
    for coefficient in ATAN[1:]:
        poly = poly * square + coefficient
    angle = poly * ratio
    angle = jnp.where(steep, np.float32(np.pi / 2) - angle, angle)
    return jnp.where(imag < 0, -angle, angle)


def cut_kernel(start, scenes_ref, *refs):
    *outs, sems = refs
    copies = []
    for k, out in enumerate(outs):
        rows = out.shape[2]
        copies.append(pltpu.make_async_copy(scenes_ref.at[:, :, pl.ds(start, rows), :], out, sems.at[k]))
        start += rows
    for copy in copies:
        copy.start()
    for copy in copies:
        copy.wait()


def cut_rows(scenes, start, sizes):
    acq, parts, _, cols = scenes.shape
    vmem = pl.BlockSpec(memory_space=pltpu.VMEM)
    return pl.pallas_call(
        functools.partial(cut_kernel, start),
        out_shape=[jax.ShapeDtypeStruct((acq, parts, rows, cols), scenes.dtype) for rows in sizes],
        in_specs=[pl.BlockSpec(memory_space=pltpu.HBM)],
        out_specs=[vmem] * len(sizes),
        scratch_shapes=[pltpu.SemaphoreType.DMA((len(sizes),))],
        compiler_params=pltpu.CompilerParams(vmem_limit_bytes=SMALL_VMEM),
        name="cut_rows",
    )(scenes)


def split(x, count):
    pieces = []
    for _ in range(count):
        pieces.append(x.astype(jnp.bfloat16))
        x = x - pieces[-1].astype(jnp.float32)
    return pieces


def phase_kernel(pairs_ref, near_ref, own_ref, far_ref, ones_ref, *refs):
    *earlier, out_ref, stack, sums = refs
    pair_count = pairs_ref.shape[0]
    acq, _, rows, cols = far_ref.shape
    bands, looked = rows // BAND, BAND // LOOK_R
    blocks = cols // LANES
    picks = [(pairs_ref[p, 0], pairs_ref[p, 1]) for p in range(pair_count)]

    def band(b, carry):
        at = pl.ds(pl.multiple_of(b * BAND, BAND), BAND)

        def widen(j, carry):
            lanes = pl.ds(pl.multiple_of(j * LANES, LANES), LANES)
            for side, ref in enumerate((far_ref, own_ref, near_ref)):
                for a in range(acq):
                    for part in range(2):
                        stack[side * acq + a, part, j] = ref[a, part, at, lanes].astype(jnp.float32)
            return carry

        def form(j, carry):
            lanes = pl.ds(pl.multiple_of(j * LANES, LANES), LANES)
            for p, (first, second) in enumerate(picks):
                real = imag = None
                for i in range(LOOK_R):
                    pick = pl.ds(i, looked, stride=LOOK_R)
                    ar, ai = stack[first, 0, j, pick, :], stack[first, 1, j, pick, :]
                    cr, ci = stack[second, 0, j, pick, :], stack[second, 1, j, pick, :]
                    re, im = ar * cr + ai * ci, ai * cr - ar * ci
                    real = re if real is None else real + re
                    imag = im if imag is None else imag + im
                for piece, value in enumerate(split(jnp.concatenate([real, imag], axis=0), 2)):
                    sums[piece, b, pl.ds(p * 2 * looked, 2 * looked), lanes] = value
            return carry

        lax.fori_loop(0, blocks, widen, 0, unroll=4)
        lax.fori_loop(0, blocks, form, 0, unroll=4)
        return carry

    lax.fori_loop(0, bands, band, 0)
    pieces = sums[...].reshape(2 * bands * sums.shape[2], cols)
    dots = jnp.dot(pieces, ones_ref[...], preferred_element_type=jnp.float32)
    dots = dots.reshape(2, bands, pair_count, 2, looked, dots.shape[1])
    both = dots[0] + dots[1]
    width = dots.shape[-1]
    angle = atan_ratio(both[:, :, 1], both[:, :, 0])
    at = 0
    for ref in earlier:
        out_ref[pl.ds(at, ref.shape[0])] = ref[...]
        at += ref.shape[0]
    for b in range(bands):
        for p in range(pair_count):
            out_ref[pl.ds(at + b * looked, looked), 0, pl.ds(p * width, width)] = angle[b, p]


def chunk_phase(pairs, far, own, near, ones, earlier=()):
    acq, parts, rows, cols = far.shape
    looked = rows // LOOK_R
    pair_count = pairs.shape[0]
    total = looked + sum(x.shape[0] for x in earlier)
    vmem = pl.BlockSpec(memory_space=pltpu.VMEM)
    return pl.pallas_call(
        phase_kernel,
        out_shape=jax.ShapeDtypeStruct((total, 1, pair_count * (cols // LOOK_C)), jnp.float32),
        in_specs=[pl.BlockSpec(memory_space=pltpu.SMEM)] + [vmem] * (4 + len(earlier)),
        out_specs=vmem,
        scratch_shapes=[
            pltpu.VMEM((3 * acq, parts, cols // LANES, BAND, LANES), jnp.float32),
            pltpu.VMEM((2, rows // BAND, 2 * pair_count * BAND // LOOK_R, cols), jnp.bfloat16),
        ],
        compiler_params=pltpu.CompilerParams(vmem_limit_bytes=PHASE_VMEM),
        name="pair_phase",
    )(pairs, near, own, far, ones, *earlier)


def constants_kernel(owner_ref, pinv_ref, slots_ref, ones_ref):
    count = pinv_ref.shape[1]
    row = lax.broadcasted_iota(jnp.int32, (count, owner_ref.shape[1]), 0)
    pick = (row == owner_ref[...]).astype(jnp.bfloat16)
    for piece, value in enumerate(split(pinv_ref[...], 3)):
        slots_ref[piece] = jnp.dot(value, pick, preferred_element_type=jnp.float32).astype(jnp.bfloat16)
    col = lax.broadcasted_iota(jnp.int32, ones_ref.shape, 0) // LOOK_C
    ones_ref[...] = (col == lax.broadcasted_iota(jnp.int32, ones_ref.shape, 1)).astype(jnp.bfloat16)


def series_kernel(slots_ref, phase_ref, out_ref):
    acqs, width = slots_ref.shape[1:]
    count, _, lanes = phase_ref.shape
    lanes = lanes * count // width
    phase = [phase_ref[:, 0, pl.ds(p * lanes, lanes)] for p in range(width // count)]
    phase = split(jnp.concatenate(phase, axis=0), 3)
    total = None
    for piece in reversed(range(3)):
        rows = slots_ref[pl.ds(0, 3 - piece)].reshape((3 - piece) * acqs, width)
        dots = jnp.dot(rows, phase[piece], preferred_element_type=jnp.float32)
        for k in reversed(range(3 - piece)):
            part = dots[k * acqs : (k + 1) * acqs]
            total = part if total is None else total + part
    out_ref[0] = total


def body(scenes, pairs, pair_owner, design_pinv):
    acq, parts, rows, cols = scenes.shape
    pair_count = pairs.shape[0]
    count = lax.axis_size("acq")
    me = lax.axis_index("acq")
    near_pairs = [(i, i ^ 1) for i in range(count)]
    far_pairs = [(i, i + 1 if i % 2 else i - 1) for i in range(1, count - 1)]
    local = pairs - (me - 1) * acq
    local = jnp.where(me % 2 == 1, (2 - local // acq) * acq + local % acq, local)

    owner = pair_owner.reshape(count, pair_count).T.reshape(1, count * pair_count)
    slots, ones = pl.pallas_call(
        constants_kernel,
        out_shape=[
            jax.ShapeDtypeStruct((3, design_pinv.shape[0], count * pair_count), jnp.bfloat16),
            jax.ShapeDtypeStruct((cols, cols // LOOK_C), jnp.bfloat16),
        ],
        compiler_params=pltpu.CompilerParams(vmem_limit_bytes=SMALL_VMEM),
        name="constants",
    )(owner, design_pinv)

    def swap(chunk):
        near = lax.ppermute(chunk, "acq", near_pairs)
        return lax.ppermute(chunk, "acq", far_pairs), near

    chunks = [lax.slice_in_dim(scenes, 0, CHUNKS[0], axis=2)]
    halos, phases = [swap(chunks[0])], []
    rest, slots, ones, chunks[0] = lax.optimization_barrier((scenes, slots, ones, chunks[0]))
    chunks += list(cut_rows(rest, CHUNKS[0], CHUNKS[1:]))
    halos.append(swap(chunks[1]))
    for k, chunk in enumerate(chunks):
        far, near = halos[k]
        last = k == len(chunks) - 1
        phases.append(chunk_phase(local, far, chunk, near, ones, phases if last else ()))
        if k + 2 < len(chunks):
            done = phases if k == 0 else halos
            chunks[k + 2], done[k] = lax.optimization_barrier((chunks[k + 2], done[k]))
            halos.append(swap(chunks[k + 2]))
    phase = lax.all_to_all(phases[-1], "acq", split_axis=0, concat_axis=0)
    return pl.pallas_call(
        series_kernel,
        out_shape=jax.ShapeDtypeStruct((1, slots.shape[1], cols // LOOK_C), jnp.float32),
        compiler_params=pltpu.CompilerParams(vmem_limit_bytes=SMALL_VMEM),
        name="series",
    )(slots, phase)


def solution(mesh):
    placed = (P("acq", None, None, "rng"), P("acq", None), P(), P())
    return jax.shard_map(
        body, mesh=mesh, in_specs=placed, out_specs=P("acq", None, "rng"), check_vma=False
    )
```

```python
import functools

import jax
import jax.numpy as jnp
import numpy as np
from jax import lax
from jax.experimental import pallas as pl
from jax.experimental.pallas import tpu as pltpu
from jax.sharding import PartitionSpec as P

LOOK_R = 4
LOOK_C = 16
LANES = 128
CHUNKS = (64, 96, 64, 32)
BAND = 32
PHASE_VMEM = 10 * 2**20
SMALL_VMEM = 6 * 2**20

ATAN = (
    0.0030499680532062342, -0.016827448459262765, 0.04385559893448732,
    -0.07596809856148054, 0.1068142102724691, -0.14213196195363814,
    0.19993716142481088, -0.33333120780995057, 0.9999999880828068,
)


def atan_ratio(imag, real):
    size = jnp.abs(imag)
    steep = size > real
    ratio = jnp.minimum(size, real) / jnp.maximum(size, real)
    square = ratio * ratio
    poly = jnp.full_like(square, ATAN[0])
    for coefficient in ATAN[1:]:
        poly = poly * square + coefficient
    angle = poly * ratio
    angle = jnp.where(steep, np.float32(np.pi / 2) - angle, angle)
    return jnp.where(imag < 0, -angle, angle)


def cut_kernel(places, scenes_ref, *refs):
    *outs, sems = refs
    copies = []
    for k, (out, (row, col)) in enumerate(zip(outs, places)):
        _, _, rows, cols = out.shape
        source = scenes_ref.at[:, :, pl.ds(row, rows), pl.ds(col, cols)]
        copies.append(pltpu.make_async_copy(source, out, sems.at[k]))
    for copy in copies:
        copy.start()
    for copy in copies:
        copy.wait()


def cut(scenes, places, sizes):
    acq, parts = scenes.shape[:2]
    vmem = pl.BlockSpec(memory_space=pltpu.VMEM)
    return pl.pallas_call(
        functools.partial(cut_kernel, places),
        out_shape=[jax.ShapeDtypeStruct((acq, parts, rows, cols), scenes.dtype) for rows, cols in sizes],
        in_specs=[pl.BlockSpec(memory_space=pltpu.HBM)],
        out_specs=[vmem] * len(sizes),
        scratch_shapes=[pltpu.SemaphoreType.DMA((len(sizes),))],
        compiler_params=pltpu.CompilerParams(vmem_limit_bytes=SMALL_VMEM),
        name="cut",
    )(scenes)


def split(x, count):
    pieces = []
    for _ in range(count):
        pieces.append(x.astype(jnp.bfloat16))
        x = x - pieces[-1].astype(jnp.float32)
    return pieces


def phase_kernel(first_col, has_partial, keep_sums, pairs_ref, near_ref, own_ref, far_ref, ones_ref, *refs):
    *earlier, out_ref, stack, sums = refs
    partial = earlier.pop() if has_partial else None
    pair_count = pairs_ref.shape[0]
    acq, _, rows, cols = far_ref.shape
    bands, looked = rows // BAND, BAND // LOOK_R
    blocks = cols // LANES
    picks = [(pairs_ref[p, 0], pairs_ref[p, 1]) for p in range(pair_count)]

    def band(b, carry):
        at = pl.ds(pl.multiple_of(b * BAND, BAND), BAND)

        def widen(j, carry):
            lanes = pl.ds(pl.multiple_of(j * LANES, LANES), LANES)
            wide = pl.ds(pl.multiple_of(first_col + j * LANES, LANES), LANES)
            for side, (ref, cut) in enumerate(((far_ref, lanes), (own_ref, wide), (near_ref, wide))):
                for a in range(acq):
                    for part in range(2):
                        stack[side * acq + a, part, j] = ref[a, part, at, cut].astype(jnp.float32)
            return carry

        def form(j, carry):
            lanes = pl.ds(pl.multiple_of(j * LANES, LANES), LANES)
            for p, (first, second) in enumerate(picks):
                real = imag = None
                for i in range(LOOK_R):
                    pick = pl.ds(i, looked, stride=LOOK_R)
                    ar, ai = stack[first, 0, j, pick, :], stack[first, 1, j, pick, :]
                    cr, ci = stack[second, 0, j, pick, :], stack[second, 1, j, pick, :]
                    re, im = ar * cr + ai * ci, ai * cr - ar * ci
                    real = re if real is None else real + re
                    imag = im if imag is None else imag + im
                for piece, value in enumerate(split(jnp.concatenate([real, imag], axis=0), 2)):
                    sums[piece, b, pl.ds(p * 2 * looked, 2 * looked), lanes] = value
            return carry

        lax.fori_loop(0, blocks, widen, 0, unroll=4)
        lax.fori_loop(0, blocks, form, 0, unroll=4)
        return carry

    lax.fori_loop(0, bands, band, 0)
    pieces = sums[...].reshape(2 * bands * sums.shape[2], cols)
    dots = jnp.dot(pieces, ones_ref[pl.ds(first_col, cols)], preferred_element_type=jnp.float32)
    dots = dots.reshape(2, bands, pair_count, 2, looked, dots.shape[1])
    both = dots[0] + dots[1]
    if partial is not None:
        both = both + partial[...].reshape(both.shape)
    if keep_sums:
        out_ref[...] = both.reshape(out_ref.shape)
        return
    angle = atan_ratio(both[:, :, 1], both[:, :, 0])
    at = 0
    for ref in earlier:
        out_ref[pl.ds(at * pair_count, ref.shape[0]), :] = ref[...]
        at += ref.shape[0] // pair_count
    for b in range(bands):
        for p in range(pair_count):
            out_ref[pl.ds((at + b * looked) * pair_count + p, looked, stride=pair_count), :] = angle[b, p]


def chunk_phase(pairs, far, own, near, ones, earlier=(), first_col=0, partial=None, keep_sums=False):
    acq, parts, rows, cols = far.shape
    looked = rows // LOOK_R
    pair_count = pairs.shape[0]
    total = pair_count * looked * (2 if keep_sums else 1) + sum(x.shape[0] for x in earlier)
    more = list(earlier) + ([] if partial is None else [partial])
    vmem = pl.BlockSpec(memory_space=pltpu.VMEM)
    return pl.pallas_call(
        functools.partial(phase_kernel, first_col, partial is not None, keep_sums),
        out_shape=jax.ShapeDtypeStruct((total, own.shape[3] // LOOK_C), jnp.float32),
        in_specs=[pl.BlockSpec(memory_space=pltpu.SMEM)] + [vmem] * (4 + len(more)),
        out_specs=vmem,
        scratch_shapes=[
            pltpu.VMEM((3 * acq, parts, cols // LANES, BAND, LANES), jnp.float32),
            pltpu.VMEM((2, rows // BAND, 2 * pair_count * BAND // LOOK_R, cols), jnp.bfloat16),
        ],
        compiler_params=pltpu.CompilerParams(vmem_limit_bytes=PHASE_VMEM),
        name="pair_phase",
    )(pairs, near, own, far, ones, *more)


def constants_kernel(owner_ref, pinv_ref, slots_ref, ones_ref):
    count = pinv_ref.shape[1]
    row = lax.broadcasted_iota(jnp.int32, (count, owner_ref.shape[1]), 0)
    pick = (row == owner_ref[...]).astype(jnp.bfloat16)
    for piece, value in enumerate(split(pinv_ref[...], 3)):
        slots_ref[piece] = jnp.dot(value, pick, preferred_element_type=jnp.float32).astype(jnp.bfloat16)
    col = lax.broadcasted_iota(jnp.int32, ones_ref.shape, 0) // LOOK_C
    ones_ref[...] = (col == lax.broadcasted_iota(jnp.int32, ones_ref.shape, 1)).astype(jnp.bfloat16)


def series_kernel(slots_ref, phase_ref, out_ref):
    acqs, width = slots_ref.shape[1:]
    phase = split(phase_ref[...], 3)
    total = None
    for piece in reversed(range(3)):
        rows = slots_ref[pl.ds(0, 3 - piece)].reshape((3 - piece) * acqs, width)
        dots = jnp.dot(rows, phase[piece], preferred_element_type=jnp.float32)
        for k in reversed(range(3 - piece)):
            part = dots[k * acqs : (k + 1) * acqs]
            total = part if total is None else total + part
    out_ref[0] = total


def body(scenes, pairs, pair_owner, design_pinv):
    acq, parts, rows, cols = scenes.shape
    pair_count = pairs.shape[0]
    count = lax.axis_size("acq")
    me = lax.axis_index("acq")
    near_pairs = [(i, i ^ 1) for i in range(count)]
    far_pairs = [(i, i + 1 if i % 2 else i - 1) for i in range(1, count - 1)]
    local = pairs - (me - 1) * acq
    local = jnp.where(me % 2 == 1, (2 - local // acq) * acq + local % acq, local)

    owner = pair_owner.reshape(1, count * pair_count)
    slots, ones = pl.pallas_call(
        constants_kernel,
        out_shape=[
            jax.ShapeDtypeStruct((3, design_pinv.shape[0], count * pair_count), jnp.bfloat16),
            jax.ShapeDtypeStruct((cols, cols // LOOK_C), jnp.bfloat16),
        ],
        compiler_params=pltpu.CompilerParams(vmem_limit_bytes=SMALL_VMEM),
        name="constants",
    )(owner, design_pinv)

    def far_of(chunk):
        return lax.ppermute(chunk, "acq", far_pairs)

    def near_of(chunk):
        return lax.ppermute(chunk, "acq", near_pairs)

    starts = [sum(CHUNKS[:k]) for k in range(len(CHUNKS))]
    half = cols // 2
    places = [(start, 0) for start in starts[1:]] + [(starts[-1], 0), (starts[-1], half)]
    sizes = [(step, cols) for step in CHUNKS[1:]] + [(CHUNKS[-1], half)] * 2
    chunks = [lax.slice_in_dim(scenes, 0, CHUNKS[0], axis=2)]
    nears, fars, phases = [near_of(chunks[0])], [far_of(chunks[0])], []
    rest, slots, ones, chunks[0] = lax.optimization_barrier((scenes, slots, ones, chunks[0]))
    *others, left, right = cut(rest, places, sizes)
    chunks += others
    nears.append(near_of(chunks[1]))
    fars.append(far_of(chunks[1]))
    for k, chunk in enumerate(chunks[:-1]):
        phases.append(chunk_phase(local, fars[k], chunk, nears[k], ones))
        if k == 0:
            chunks[2], phases[0] = lax.optimization_barrier((chunks[2], phases[0]))
            nears.append(near_of(chunks[2]))
            fars.append(far_of(chunks[2]))
            chunks[3], left, right, nears[2] = lax.optimization_barrier((chunks[3], left, right, nears[2]))
            nears.append(near_of(chunks[3]))
            fars += [far_of(left), far_of(right)]
    part = chunk_phase(local, fars[3], chunks[3], nears[3], ones, keep_sums=True)
    phases.append(chunk_phase(local, fars[4], chunks[3], nears[3], ones, phases, half, part))
    phase = lax.all_to_all(phases[-1].reshape(count, 1, -1), "acq", split_axis=0, concat_axis=0)
    phase = phase.reshape(count * pair_count, -1)
    return pl.pallas_call(
        series_kernel,
        out_shape=jax.ShapeDtypeStruct((1, slots.shape[1], cols // LOOK_C), jnp.float32),
        compiler_params=pltpu.CompilerParams(vmem_limit_bytes=SMALL_VMEM),
        name="series",
    )(slots, phase)


def solution(mesh):
    placed = (P("acq", None, None, "rng"), P("acq", None), P(), P())
    return jax.shard_map(
        body, mesh=mesh, in_specs=placed, out_specs=P("acq", None, "rng"), check_vma=False
    )
```

```python
import functools

import jax
import jax.numpy as jnp
import numpy as np
from jax import lax
from jax.experimental import pallas as pl
from jax.experimental.pallas import tpu as pltpu
from jax.sharding import PartitionSpec as P

LOOK_R = 4
LOOK_C = 16
LANES = 128
CHUNKS = (64, 96, 64, 32)
BAND = 32
PHASE_VMEM = 10 * 2**20
SMALL_VMEM = 6 * 2**20

ATAN = (
    0.0030499680532062342, -0.016827448459262765, 0.04385559893448732,
    -0.07596809856148054, 0.1068142102724691, -0.14213196195363814,
    0.19993716142481088, -0.33333120780995057, 0.9999999880828068,
)


def atan_ratio(imag, real):
    size = jnp.abs(imag)
    steep = size > real
    ratio = jnp.minimum(size, real) / jnp.maximum(size, real)
    square = ratio * ratio
    poly = jnp.full_like(square, ATAN[0])
    for coefficient in ATAN[1:]:
        poly = poly * square + coefficient
    angle = poly * ratio
    angle = jnp.where(steep, np.float32(np.pi / 2) - angle, angle)
    return jnp.where(imag < 0, -angle, angle)


def cut_kernel(places, scenes_ref, *refs):
    *outs, sems = refs
    copies = []
    for k, (out, (row, col)) in enumerate(zip(outs, places)):
        _, _, rows, cols = out.shape
        source = scenes_ref.at[:, :, pl.ds(row, rows), pl.ds(col, cols)]
        copies.append(pltpu.make_async_copy(source, out, sems.at[k]))
    for copy in copies:
        copy.start()
    for copy in copies:
        copy.wait()


def cut(scenes, places, sizes):
    acq, parts = scenes.shape[:2]
    vmem = pl.BlockSpec(memory_space=pltpu.VMEM)
    return pl.pallas_call(
        functools.partial(cut_kernel, places),
        out_shape=[jax.ShapeDtypeStruct((acq, parts, rows, cols), scenes.dtype) for rows, cols in sizes],
        in_specs=[pl.BlockSpec(memory_space=pltpu.HBM)],
        out_specs=[vmem] * len(sizes),
        scratch_shapes=[pltpu.SemaphoreType.DMA((len(sizes),))],
        compiler_params=pltpu.CompilerParams(vmem_limit_bytes=SMALL_VMEM),
        name="cut",
    )(scenes)


def split(x, count):
    pieces = []
    for _ in range(count):
        pieces.append(x.astype(jnp.bfloat16))
        x = x - pieces[-1].astype(jnp.float32)
    return pieces


def phase_kernel(first_col, has_partial, keep_sums, pairs_ref, near_ref, own_ref, far_ref, ones_ref, *refs):
    *earlier, out_ref, stack, sums = refs
    partial = earlier.pop() if has_partial else None
    pair_count = pairs_ref.shape[0]
    acq, _, rows, cols = far_ref.shape
    bands, looked = rows // BAND, BAND // LOOK_R
    blocks = cols // LANES
    picks = [(pairs_ref[p, 0], pairs_ref[p, 1]) for p in range(pair_count)]

    def band(b, carry):
        at = pl.ds(pl.multiple_of(b * BAND, BAND), BAND)

        def widen(j, carry):
            lanes = pl.ds(pl.multiple_of(j * LANES, LANES), LANES)
            wide = pl.ds(pl.multiple_of(first_col + j * LANES, LANES), LANES)
            for side, (ref, cut) in enumerate(((far_ref, lanes), (own_ref, wide), (near_ref, wide))):
                for a in range(acq):
                    for part in range(2):
                        stack[side * acq + a, part, j] = ref[a, part, at, cut].astype(jnp.float32)
            return carry

        def form(j, carry):
            lanes = pl.ds(pl.multiple_of(j * LANES, LANES), LANES)
            for p, (first, second) in enumerate(picks):
                real = imag = None
                for i in range(LOOK_R):
                    pick = pl.ds(i, looked, stride=LOOK_R)
                    ar, ai = stack[first, 0, j, pick, :], stack[first, 1, j, pick, :]
                    cr, ci = stack[second, 0, j, pick, :], stack[second, 1, j, pick, :]
                    re, im = ar * cr + ai * ci, ai * cr - ar * ci
                    real = re if real is None else real + re
                    imag = im if imag is None else imag + im
                for piece, value in enumerate(split(jnp.concatenate([real, imag], axis=0), 2)):
                    sums[piece, b, pl.ds(p * 2 * looked, 2 * looked), lanes] = value
            return carry

        lax.fori_loop(0, blocks, widen, 0, unroll=4)
        lax.fori_loop(0, blocks, form, 0, unroll=4)
        return carry

    lax.fori_loop(0, bands, band, 0)
    pieces = sums[...].reshape(2 * bands * sums.shape[2], cols)
    dots = jnp.dot(pieces, ones_ref[pl.ds(first_col, cols)], preferred_element_type=jnp.float32)
    dots = dots.reshape(2, bands, pair_count, 2, looked, dots.shape[1])
    both = dots[0] + dots[1]
    if partial is not None:
        both = both + partial[...].reshape(both.shape)
    if keep_sums:
        out_ref[...] = both.reshape(out_ref.shape)
        return
    angle = atan_ratio(both[:, :, 1], both[:, :, 0])
    at = 0
    for ref in earlier:
        out_ref[pl.ds(at * pair_count, ref.shape[0]), :] = ref[...]
        at += ref.shape[0] // pair_count
    for b in range(bands):
        for p in range(pair_count):
            out_ref[pl.ds((at + b * looked) * pair_count + p, looked, stride=pair_count), :] = angle[b, p]


def chunk_phase(pairs, far, own, near, ones, earlier=(), first_col=0, partial=None, keep_sums=False):
    acq, parts, rows, cols = far.shape
    looked = rows // LOOK_R
    pair_count = pairs.shape[0]
    total = pair_count * looked * (2 if keep_sums else 1) + sum(x.shape[0] for x in earlier)
    more = list(earlier) + ([] if partial is None else [partial])
    vmem = pl.BlockSpec(memory_space=pltpu.VMEM)
    return pl.pallas_call(
        functools.partial(phase_kernel, first_col, partial is not None, keep_sums),
        out_shape=jax.ShapeDtypeStruct((total, own.shape[3] // LOOK_C), jnp.float32),
        in_specs=[vmem] * (5 + len(more)),
        out_specs=vmem,
        scratch_shapes=[
            pltpu.VMEM((3 * acq, parts, cols // LANES, BAND, LANES), jnp.float32),
            pltpu.VMEM((2, rows // BAND, 2 * pair_count * BAND // LOOK_R, cols), jnp.bfloat16),
        ],
        compiler_params=pltpu.CompilerParams(vmem_limit_bytes=PHASE_VMEM),
        name="pair_phase",
    )(pairs, near, own, far, ones, *more)


def constants_kernel(owner_ref, pinv_ref, slots_ref, ones_ref):
    count = pinv_ref.shape[1]
    row = lax.broadcasted_iota(jnp.int32, (count, owner_ref.shape[1]), 0)
    pick = (row == owner_ref[...]).astype(jnp.bfloat16)
    for piece, value in enumerate(split(pinv_ref[...], 3)):
        slots_ref[piece] = jnp.dot(value, pick, preferred_element_type=jnp.float32).astype(jnp.bfloat16)
    col = lax.broadcasted_iota(jnp.int32, ones_ref.shape, 0) // LOOK_C
    ones_ref[...] = (col == lax.broadcasted_iota(jnp.int32, ones_ref.shape, 1)).astype(jnp.bfloat16)


def series_kernel(slots_ref, phase_ref, out_ref):
    acqs, width = slots_ref.shape[1:]
    phase = split(phase_ref[...], 3)
    total = None
    for piece in reversed(range(3)):
        rows = slots_ref[pl.ds(0, 3 - piece)].reshape((3 - piece) * acqs, width)
        dots = jnp.dot(rows, phase[piece], preferred_element_type=jnp.float32)
        for k in reversed(range(3 - piece)):
            part = dots[k * acqs : (k + 1) * acqs]
            total = part if total is None else total + part
    out_ref[0] = total


def body(scenes, pairs, pair_owner, design_pinv):
    acq, parts, rows, cols = scenes.shape
    pair_count = pairs.shape[0]
    count = lax.axis_size("acq")
    me = lax.axis_index("acq")
    near_pairs = [(i, i ^ 1) for i in range(count)]
    far_pairs = [(i, i + 1 if i % 2 else i - 1) for i in range(1, count - 1)]
    local = pairs - (me - 1) * acq
    local = jnp.where(me % 2 == 1, (2 - local // acq) * acq + local % acq, local)

    owner = pair_owner.reshape(1, count * pair_count)
    slots, ones = pl.pallas_call(
        constants_kernel,
        out_shape=[
            jax.ShapeDtypeStruct((3, design_pinv.shape[0], count * pair_count), jnp.bfloat16),
            jax.ShapeDtypeStruct((cols, cols // LOOK_C), jnp.bfloat16),
        ],
        compiler_params=pltpu.CompilerParams(vmem_limit_bytes=SMALL_VMEM),
        name="constants",
    )(owner, design_pinv)

    def far_of(chunk):
        return lax.ppermute(chunk, "acq", far_pairs)

    def near_of(chunk):
        return lax.ppermute(chunk, "acq", near_pairs)

    starts = [sum(CHUNKS[:k]) for k in range(len(CHUNKS))]
    half = cols // 2
    places = [(start, 0) for start in starts[1:]] + [(starts[-1], 0), (starts[-1], half)]
    sizes = [(step, cols) for step in CHUNKS[1:]] + [(CHUNKS[-1], half)] * 2
    chunks = [lax.slice_in_dim(scenes, 0, CHUNKS[0], axis=2)]
    nears, fars, phases = [near_of(chunks[0])], [far_of(chunks[0])], []
    rest, slots, ones, chunks[0] = lax.optimization_barrier((scenes, slots, ones, chunks[0]))
    *others, left, right = cut(rest, places, sizes)
    chunks += others
    nears.append(near_of(chunks[1]))
    fars.append(far_of(chunks[1]))
    for k, chunk in enumerate(chunks[:-1]):
        phases.append(chunk_phase(local, fars[k], chunk, nears[k], ones))
        if k == 0:
            chunks[2], phases[0] = lax.optimization_barrier((chunks[2], phases[0]))
            nears.append(near_of(chunks[2]))
            fars.append(far_of(chunks[2]))
            chunks[3], left, right, nears[2] = lax.optimization_barrier((chunks[3], left, right, nears[2]))
            nears.append(near_of(chunks[3]))
            fars += [far_of(left), far_of(right)]
    part = chunk_phase(local, fars[3], chunks[3], nears[3], ones, keep_sums=True)
    phases.append(chunk_phase(local, fars[4], chunks[3], nears[3], ones, phases, half, part))
    phase = lax.all_to_all(phases[-1].reshape(count, 1, -1), "acq", split_axis=0, concat_axis=0)
    phase = phase.reshape(count * pair_count, -1)
    return pl.pallas_call(
        series_kernel,
        out_shape=jax.ShapeDtypeStruct((1, slots.shape[1], cols // LOOK_C), jnp.float32),
        compiler_params=pltpu.CompilerParams(vmem_limit_bytes=SMALL_VMEM),
        name="series",
    )(slots, phase)


def solution(mesh):
    placed = (P("acq", None, None, "rng"), P("acq", None), P(), P())
    return jax.shard_map(
        body, mesh=mesh, in_specs=placed, out_specs=P("acq", None, "rng"), check_vma=False
    )
```
